512 devices in a mesh: pts: 64 (over z, x), cand: 8 (over y, core).
Axes of the slice: x: 4, y: 4, z: 16, core: 2. Of those that a mesh axis runs over, the one named last changes fastest.
Arguments:
- points: float32 [131072, 512], P('pts'), may hold values from -10 to 10
- prior_min: float32 [131072], P('pts'), may hold values from 0.05 to 6
- cand_slots: int32 [64, 8, 32], P('pts', 'cand'), may hold values from -1 to 2047, as said below
Outputs:
- new_min: float32 [131072], P('pts')
- cost: float32 [], replicated
The draws below stay inside these ranges and needn't reach their ends.
Inputs may be any that keep to these rules, and one draw needn't show every extreme that they name: `cand_slots`: in each [o, b] row the live entries come first, 1 to 32 of them, and are distinct local rows, distinct over all b of one owner; some [o, b] row is full.
All inputs are finite; a program needn't handle non-finite values.
Results may differ from the reference program's by a relative error of at most 0.0003.
Values sent between devices are 32-bit elements; how exact they have to be, the bound alone decides.
A program may use at most 64 MiB of HBM per device.

```python
import jax
import jax.numpy as jnp
from jax import lax

D = 512
PTS_DEV = 2048
CAP = 32
OWNERS = 64
CSHARDS = 8
NPTS = 131072


def draw_points(key, part):
    key = jax.random.fold_in(key, 7)
    key_centres, key_assign, key_jitter, key_spread = jax.random.split(key, 4)
    clusters = max(NPTS // 32, 4)
    cluster_ids = jax.random.randint(key_assign, (NPTS,), 0, clusters)
    owner = (jnp.arange(NPTS) // PTS_DEV).astype(jnp.float32)
    owner_span = max(OWNERS - 1, 1)
    centres = jax.random.normal(key_centres, (clusters, D), jnp.float32)
    jitter = jax.random.normal(key_jitter, (NPTS, D), jnp.float32)
    spread = jnp.exp(jax.random.uniform(key_spread, (NPTS,), jnp.float32, jnp.log(0.01), jnp.log(0.1)))
    growth = 1.0 + 8.0 * owner / owner_span
    noise_scale = jnp.sqrt(spread * growth)
    drawn = jnp.take(centres, cluster_ids, axis=0) + jitter * noise_scale[:, None]
    return jnp.clip(drawn, -10.0, 10.0).astype(jnp.float32)


def draw_prior_min(key, part):
    key = jax.random.fold_in(key, 11)
    owner = (jnp.arange(NPTS) // PTS_DEV).astype(jnp.float32)
    owner_span = max(OWNERS - 1, 1)
    levels = jnp.exp(jax.random.uniform(key, (NPTS,), jnp.float32, jnp.log(0.05), jnp.log(1.5)))
    growth = 1.0 + 2.0 * owner / owner_span
    return jnp.clip(levels * growth, 0.05, 6.0).astype(jnp.float32)


def draw_cand_slots(key, part):
    key = jax.random.fold_in(key, 5)
    first, second, third = jax.random.split(key, 3)
    keys = jax.random.split(first, OWNERS)
    perm = jax.vmap(lambda k: jax.random.permutation(k, PTS_DEV))(keys)
    perm = perm[:, :CSHARDS * CAP].reshape(OWNERS, CSHARDS, CAP)
    counts = jax.random.randint(second, (OWNERS, CSHARDS), 1, CAP + 1)
    pick = jax.random.randint(third, (), 0, OWNERS * CSHARDS)
    flat = jnp.arange(OWNERS * CSHARDS).reshape(OWNERS, CSHARDS)
    counts = jnp.where(flat == pick, CAP, counts)
    live = jnp.arange(CAP)[None, None, :] < counts[:, :, None]
    return jnp.where(live, perm, -1).astype(jnp.int32)


def setup_inputs(seed: int = 0) -> dict:
    seeds = jax.random.split(jax.random.key(seed), 4)
    return {
        "points": draw_points(jax.random.fold_in(seeds[3], 71), 0),
        "prior_min": draw_prior_min(jax.random.fold_in(seeds[3], 71), 0),
        "cand_slots": draw_cand_slots(jax.random.fold_in(seeds[3], 71), 0),
    }


def reference(points, prior_min, cand_slots):
    owner = jnp.arange(OWNERS, dtype=jnp.int32)[:, None, None]
    live = cand_slots >= 0
    index = (owner * PTS_DEV + jnp.maximum(cand_slots, 0)).astype(jnp.int32).reshape(-1)
    live = live.reshape(-1)
    rows = jnp.take(points, index, axis=0) * live[:, None].astype(jnp.float32)
    cnorm = jnp.where(live, jnp.sum(rows * rows, axis=1), jnp.float32(1e30))
    blocks = points.reshape(NPTS // PTS_DEV, PTS_DEV, D)

    def nearest(block):
        pnorm = jnp.sum(block * block, axis=1)
        dots = jnp.dot(block, rows.T, precision=lax.Precision.HIGHEST, preferred_element_type=jnp.float32)
        dist = (pnorm[:, None] + cnorm[None, :] - 2.0 * dots) / D
        return jnp.min(dist, axis=1)

    found = lax.map(nearest, blocks).reshape(-1)
    new_min = jnp.minimum(prior_min, found)
    cost = jnp.sum(new_min) / NPTS
    return new_min, cost
```

```python
import functools

import jax
import jax.numpy as jnp
from jax import lax
from jax.experimental import pallas as pl
from jax.experimental.pallas import tpu as pltpu
from jax.sharding import PartitionSpec as P

MESH = pl.DeviceIdType.MESH
NX, NZ, NC = 4, 16, 8
HALF = NZ // 2
RA, RB = 8, 24
F32, BF16 = jnp.float32, jnp.bfloat16


def kernel(
    pts_hbm, prior_ref, slots_ref, out_ref, cost_ref,
    pf, p3, pn, ga, gb, c3, cnb, acc, mins, sx, sz,
    load_sem, ssem, rbz, raz, rx, rr, rax, rbx, s0, scm, rcm, scx, rcx, scz, rcz,
):
    p, c = lax.axis_index("pts"), lax.axis_index("cand")
    z, x = p // NX, p % NX
    npts, width = pf.shape
    quarter = npts // 4

    def peer(dz, dx):
        return (lax.rem(z + dz + NZ, NZ) * NX + lax.rem(x + dx + NX, NX), c)

    def mate(j):
        return (p, lax.rem(c + j, NC))

    def remote(src, dst, send, recv, where):
        return pltpu.make_async_remote_copy(
            src_ref=src, dst_ref=dst, send_sem=send, recv_sem=recv,
            device_id=where, device_id_type=MESH,
        )

    loads = []
    for q in range(4):
        rows = pl.ds(q * quarter, quarter)
        load = pltpu.make_async_copy(pts_hbm.at[rows], pf.at[rows], load_sem.at[q])
        load.start()
        loads.append(load)

    barrier = pltpu.get_barrier_semaphore()
    near = [peer(1, 0), peer(-1, 0), peer(0, 1), peer(0, -1), peer(0, 2)]
    near += [mate(j) for j in range(1, NC)]
    for who in near:
        pl.semaphore_signal(barrier, inc=1, device_id=who, device_id_type=MESH)
    acc[...] = jnp.full(acc.shape, 3e38, F32)
    for load in loads:
        load.wait()
    pl.semaphore_wait(barrier, len(near))

    first = slots_ref[0]
    for i in range(RA + RB):
        slot = slots_ref[i]
        row = pf[pl.ds(jnp.where(slot >= 0, slot, first), 1), :]
        if i < RA:
            ga[0, 0, i : i + 1, :] = row
        else:
            gb[0, 0, i - RA : i - RA + 1, :] = row

    def up(t):
        return jnp.maximum(2 * t - 1, 0)

    def bz_up(t):
        return remote(gb.at[0, up(t)], gb.at[0, 2 * t + 1], ssem.at[0], rbz.at[0, t + 1], peer(-1, 0))

    def bz_dn(t):
        return remote(gb.at[0, 2 * t], gb.at[0, 2 * t + 2], ssem.at[1], rbz.at[1, t + 1], peer(1, 0))

    def az_up(t):
        return remote(ga.at[up(t)], ga.at[2 * t + 1], ssem.at[2], raz.at[0, t + 1], peer(-1, 0))

    def az_dn(t):
        return remote(ga.at[2 * t], ga.at[2 * t + 2], ssem.at[3], raz.at[1, t + 1], peer(1, 0))

    def xr(t):
        two = pl.ds(2 * t - 1, 2)
        return remote(gb.at[0, two], gb.at[3, two], ssem.at[4], rx.at[0, t], peer(0, 1))

    def xl(t):
        two = pl.ds(2 * t - 1, 2)
        return remote(gb.at[0, two], gb.at[1, two], ssem.at[5], rx.at[1, t], peer(0, -1))

    def rel_r(t):
        return remote(gb.at[3, 2 * t - 1], gb.at[2, 2 * t - 1], ssem.at[6], rr.at[0, t], peer(0, 1))

    def rel_l(t):
        return remote(gb.at[1, 2 * t], gb.at[2, 2 * t], ssem.at[7], rr.at[1, t], peer(0, -1))

    own_a = [
        remote(ga.at[0, 0], ga.at[0, d], s0.at[i], rax.at[i], peer(0, -d))
        for i, d in enumerate((3, 1, 2))
    ]
    own_b = [
        remote(gb.at[0, 0], gb.at[d, 0], s0.at[3 + i], rbx.at[i], peer(0, -d))
        for i, d in enumerate((3, 1, 2))
    ]
    last_b = [
        remote(gb.at[0, 15], gb.at[d, 15], s0.at[6 + i], rbx.at[3 + i], peer(0, -d))
        for i, d in enumerate((3, 1, 2))
    ]

    bz_up(0).start()
    bz_dn(0).start()
    for copy in own_a:
        copy.start()
    for copy in own_b:
        copy.start()

    for q in range(npts // 256):
        cols = pl.ds(q * 256, 256)
        t = pf[cols, :].T
        pn[:, cols] = jnp.sum(t * t, axis=0, keepdims=True)
        t = t * -2.0
        hi = t.astype(BF16)
        lo = (t - hi.astype(F32)).astype(BF16)
        p3[0:width, cols] = hi
        p3[width : 2 * width, cols] = lo
        p3[2 * width : 3 * width, cols] = hi

    for copy in own_a:
        copy.wait_recv()
    az_up(0).start()
    az_dn(0).start()
    for copy in own_b:
        copy.wait_recv()

    def fill(at, pieces):
        rows = pieces[0] if len(pieces) == 1 else jnp.concatenate(pieces, axis=0)
        n = rows.shape[0]
        sq = rows * rows
        sq = sum(sq[:, 128 * i : 128 * i + 128] for i in range(width // 128))
        cnb[at : at + n, :] = jnp.broadcast_to(jnp.sum(sq, axis=1, keepdims=True), (n, 128))
        hi = rows.astype(BF16)
        c3[at : at + n, 0:width] = hi
        c3[at : at + n, width : 2 * width] = hi
        c3[at : at + n, 2 * width : 3 * width] = (rows - hi.astype(F32)).astype(BF16)

    def nearest(n):
        d = jnp.dot(c3[0:n, :], p3[...], preferred_element_type=F32)
        d = d + jnp.concatenate([cnb[0:n, :]] * (npts // 128), axis=1)
        acc[...] = jnp.minimum(acc[...], jnp.min(d.reshape(n // 8, 8, npts), axis=0))

    fill(112, [gb[0, 0], gb[1, 0], gb[2, 0], gb[3, 0]])
    fill(208, [ga[0].reshape(NX * RA, width), ga[0, 0], ga[0, 0]])

    def tick(t, _):
        bz_up(t - 1).wait_recv()

        @pl.when(t < HALF)
        def _():
            bz_dn(t - 1).wait_recv()

        bz_up(t - 1).wait_send()

        @pl.when(t < HALF)
        def _():
            bz_dn(t - 1).wait_send()

        @pl.when(t < HALF)
        def _():
            bz_up(t).start()

        @pl.when(t < HALF - 1)
        def _():
            bz_dn(t).start()

        @pl.when(t > 1)
        def _():
            xr(t - 1).wait_send()
            xl(t - 1).wait_send()

        @pl.when(t < HALF)
        def _():
            xr(t).start()
            xl(t).start()

        @pl.when(t == HALF)
        def _():
            for copy in last_b:
                copy.start()

        az_dn(t - 1).wait_recv()

        @pl.when(t < HALF)
        def _():
            az_up(t - 1).wait_recv()

        @pl.when(t < HALF)
        def _():
            az_up(t - 1).wait_send()

        az_dn(t - 1).wait_send()

        @pl.when(t < HALF)
        def _():
            az_dn(t).start()

        @pl.when(t < HALF - 1)
        def _():
            az_up(t).start()

        @pl.when(t >= 2)
        def _():
            xr(t - 1).wait_recv()
            xl(t - 1).wait_recv()

        @pl.when(t >= 3)
        def _():
            rel_r(t - 2).wait_send()
            rel_l(t - 2).wait_send()

        @pl.when(t >= 2)
        def _():
            rel_r(t - 1).start()
            rel_l(t - 1).start()

        @pl.when(t >= 3)
        def _():
            rel_r(t - 2).wait_recv()
            rel_l(t - 2).wait_recv()

        @pl.when(t < HALF)
        def _():
            fill(0, [ga[2 * t - 1].reshape(NX * RA, width), ga[2 * t].reshape(NX * RA, width)])
            fill(64, [gb[0, 2 * t - 1], gb[0, 2 * t]])

        @pl.when(t == HALF)
        def _():
            fill(32, [ga[2 * HALF].reshape(NX * RA, width)])
            fill(64, [gb[0, 15], gb[0, 15]])

        @pl.when(t >= 2)
        def _():
            fill(112, [gb[3, 2 * t - 3], gb[3, 2 * t - 2], gb[1, 2 * t - 3], gb[1, 2 * t - 2]])

        @pl.when(t >= 3)
        def _():
            fill(208, [gb[2, 2 * t - 5], gb[2, 2 * t - 4]])

        nearest(256)
        return 0

    lax.fori_loop(1, HALF + 1, tick, 0)

    for copy in own_a + own_b:
        copy.wait_send()
    rel_r(HALF - 1).wait_send()
    rel_l(HALF - 1).wait_send()
    rel_r(HALF - 1).wait_recv()
    rel_l(HALF - 1).wait_recv()
    for copy in last_b:
        copy.wait_recv()
    fill(0, [gb[2, 13], gb[2, 14], gb[1, 15], gb[3, 15], gb[2, 15], gb[2, 15, 0:8]])
    nearest(128)

    low = jnp.min(acc[...], axis=0, keepdims=True)
    low = (low + pn[...]) / width
    for i in range(npts // 128):
        mins[0, i : i + 1, :] = low[:, 128 * i : 128 * i + 128]
    swaps = [remote(mins.at[0], mins.at[j], scm.at[j], rcm.at[j], mate(j)) for j in range(1, NC)]
    for copy in swaps:
        copy.start()
    for copy in last_b:
        copy.wait_send()
    new = jnp.minimum(prior_ref[...], mins[0])
    for copy in swaps:
        copy.wait_recv()
    for j in range(1, NC):
        new = jnp.minimum(new, mins[j])
    out_ref[...] = new

    sx[x] = jnp.sum(new, axis=0, keepdims=True)
    sums = [
        remote(sx.at[x], sx.at[x], scx.at[d], rcx.at[d], peer(0, d)) for d in range(1, NX)
    ]
    for copy in sums:
        copy.start()
    for copy in swaps:
        copy.wait_send()
    for d in range(1, NX):
        src = lax.rem(x - d + NX, NX)
        remote(sx.at[x], sx.at[src], scx.at[d], rcx.at[d], peer(0, d)).wait_recv()
    sz[z] = (sx[0] + sx[1]) + (sx[2] + sx[3])
    sumz = [
        remote(sz.at[z], sz.at[z], scz.at[d], rcz.at[d], peer(d, 0)) for d in range(1, NZ)
    ]
    for copy in sumz:
        copy.start()
    for copy in sums:
        copy.wait_send()
    for d in range(1, NZ):
        src = lax.rem(z - d + NZ, NZ)
        remote(sz.at[z], sz.at[src], scz.at[d], rcz.at[d], peer(d, 0)).wait_recv()
    total = sz[0]
    for i in range(1, NZ):
        total = total + sz[i]
    cost_ref[...] = jnp.broadcast_to(
        jnp.sum(total, axis=1, keepdims=True) / (npts * NZ * NX), cost_ref.shape
    )
    for copy in sumz:
        copy.wait_send()


def local(points, prior_min, cand_slots):
    npts, width = points.shape
    vmem = pl.BlockSpec(memory_space=pltpu.VMEM)
    dma = pltpu.SemaphoreType.DMA
    new, cost = pl.pallas_call(
        kernel,
        out_shape=(
            jax.ShapeDtypeStruct((npts // 128, 128), F32),
            jax.ShapeDtypeStruct((1, 128), F32),
        ),
        in_specs=[
            pl.BlockSpec(memory_space=pl.ANY), vmem, pl.BlockSpec(memory_space=pltpu.SMEM),
        ],
        out_specs=(vmem, vmem),
        scratch_shapes=[
            pltpu.VMEM((npts, width), F32),
            pltpu.VMEM((3 * width, npts), BF16),
            pltpu.VMEM((1, npts), F32),
            pltpu.VMEM((NZ + 1, NX, RA, width), F32),
            pltpu.VMEM((NX, NZ, RB, width), F32),
            pltpu.VMEM((256, 3 * width), BF16),
            pltpu.VMEM((256, 128), F32),
            pltpu.VMEM((8, npts), F32),
            pltpu.VMEM((NC, npts // 128, 128), F32),
            pltpu.VMEM((NX, 1, 128), F32),
            pltpu.VMEM((NZ, 1, 128), F32),
            dma((4,)), dma((8,)),
            dma((2, HALF + 1)), dma((2, HALF + 1)), dma((2, HALF + 1)), dma((2, HALF + 1)),
            dma((3,)), dma((6,)), dma((9,)),
            dma((NC,)), dma((NC,)), dma((NX,)), dma((NX,)), dma((NZ,)), dma((NZ,)),
        ],
        compiler_params=pltpu.CompilerParams(
            collective_id=0, has_side_effects=True, vmem_limit_bytes=48 << 20
        ),
    )(points, prior_min.reshape(npts // 128, 128), cand_slots.reshape(-1))
    return new.reshape(-1), cost[0, 0]


def solution(mesh):
    placed = (P("pts", None), P("pts"), P("pts", "cand", None))
    return jax.shard_map(
        local, mesh=mesh, in_specs=placed, out_specs=(P("pts"), P()), check_vma=False
    )
```

```python
import functools

import jax
import jax.numpy as jnp
from jax import lax
from jax.experimental import pallas as pl
from jax.experimental.pallas import tpu as pltpu
from jax.sharding import PartitionSpec as P

MESH = pl.DeviceIdType.MESH
NX, NZ, NC = 4, 16, 8
HALF = NZ // 2
RA, RB = 8, 24
SPLIT = 2
F32, BF16 = jnp.float32, jnp.bfloat16


def kernel(
    pts_hbm, prior_hbm, slots_hbm, out_ref, cost_ref,
    slots_ref, prior_ref, pf, p3, pn, own, ga, gb, c3, cnb, acc, mins, sx, sz,
    load_sem, ssem, rown, rall, rx, rr, rax, rbx, s0, scm, rcm, scx, rcx, scz, rcz,
):
    p, c = lax.axis_index("pts"), lax.axis_index("cand")
    z, x = p // NX, p % NX
    npts, width = pf.shape
    quarter = npts // 4

    def peer(dz, dx):
        return (lax.rem(z + dz + NZ, NZ) * NX + lax.rem(x + dx + NX, NX), c)

    def mate(j):
        return (p, lax.rem(c + j, NC))

    def remote(src, dst, send, recv, where):
        return pltpu.make_async_remote_copy(
            src_ref=src, dst_ref=dst, send_sem=send, recv_sem=recv,
            device_id=where, device_id_type=MESH,
        )

    loads = []
    for q in range(4):
        rows = pl.ds(q * quarter, quarter)
        load = pltpu.make_async_copy(pts_hbm.at[rows], pf.at[rows], load_sem.at[q])
        load.start()
        loads.append(load)

    barrier = pltpu.get_barrier_semaphore()
    near = [peer(1, 0), peer(-1, 0), peer(0, 1), peer(0, -1), peer(0, 2)]
    near += [mate(j) for j in range(1, NC)]
    for who in near:
        pl.semaphore_signal(barrier, inc=1, device_id=who, device_id_type=MESH)
    slots_copy = pltpu.make_async_copy(slots_hbm, slots_ref, load_sem.at[4])
    slots_copy.start()
    prior_copy = pltpu.make_async_copy(prior_hbm, prior_ref, load_sem.at[5])
    prior_copy.start()
    acc[...] = jnp.full(acc.shape, 3e38, F32)
    slots_copy.wait()
    prior_copy.wait()
    for load in loads:
        load.wait()

    first = slots_ref[0]
    for i in range(RA + RB):
        slot = slots_ref[i]
        own[0, i : i + 1, :] = pf[pl.ds(jnp.where(slot >= 0, slot, first), 1), :]

    pl.semaphore_wait(barrier, len(near))

    def up(t):
        return jnp.maximum(2 * t - 1, 0)

    def sent(kind, t):
        return ssem.at[kind, lax.rem(t, 2)]

    parts = [pl.ds(i * (RA + RB) // SPLIT, (RA + RB) // SPLIT) for i in range(SPLIT)]

    def own_up(i, t):
        src, dst = own.at[up(t), parts[i]], own.at[2 * t + 1, parts[i]]
        return remote(src, dst, sent(i, t), rown.at[i, 0, t + 1], peer(-1, 0))

    def own_dn(i, t):
        src, dst = own.at[2 * t, parts[i]], own.at[2 * t + 2, parts[i]]
        return remote(src, dst, sent(2 + i, t), rown.at[i, 1, t + 1], peer(1, 0))

    def all_up(t):
        return remote(ga.at[up(t)], ga.at[2 * t + 1], sent(4, t), rall.at[0, t + 1], peer(-1, 0))

    def all_dn(t):
        return remote(ga.at[2 * t], ga.at[2 * t + 2], sent(5, t), rall.at[1, t + 1], peer(1, 0))

    def xr(t):
        two = pl.ds(2 * t - 1, 2)
        src = own.at[two, pl.ds(RA, RB)]
        return remote(src, gb.at[2, two], sent(6, t), rx.at[0, t], peer(0, 1))

    def xl(t):
        two = pl.ds(2 * t - 1, 2)
        src = own.at[two, pl.ds(RA, RB)]
        return remote(src, gb.at[0, two], sent(7, t), rx.at[1, t], peer(0, -1))

    def rel_r(t):
        at = 2 * t - 1
        return remote(gb.at[2, at], gb.at[1, at], sent(8, t), rr.at[0, t], peer(0, 1))

    def rel_l(t):
        return remote(gb.at[0, 2 * t], gb.at[1, 2 * t], sent(9, t), rr.at[1, t], peer(0, -1))

    around = (3, 1, 2)
    own_a = [
        remote(own.at[0, pl.ds(0, RA)], ga.at[0, d - 1], s0.at[i], rax.at[i], peer(0, -d))
        for i, d in enumerate(around)
    ]
    own_b = [
        remote(own.at[0, pl.ds(RA, RB)], gb.at[d - 1, 0], s0.at[3 + i], rbx.at[i], peer(0, -d))
        for i, d in enumerate(around)
    ]
    far = 2 * HALF - 1
    last_b = [
        remote(own.at[far, pl.ds(RA, RB)], gb.at[d - 1, far], s0.at[6 + i], rbx.at[3 + i], peer(0, -d))
        for i, d in enumerate(around)
    ]

    for copy in own_a:
        copy.start()
    for i in range(SPLIT):
        own_up(i, 0).start()
        own_dn(i, 0).start()
    for copy in own_b:
        copy.start()

    for q in range(npts // 256):
        cols = pl.ds(q * 256, 256)
        t = pf[cols, :].T
        pn[:, cols] = jnp.sum(t * t, axis=0, keepdims=True)
        t = t * -2.0
        hi = t.astype(BF16)
        lo = (t - hi.astype(F32)).astype(BF16)
        p3[0:width, cols] = hi
        p3[width : 2 * width, cols] = lo
        p3[2 * width : 3 * width, cols] = hi

    def fill(at, pieces):
        rows = pieces[0] if len(pieces) == 1 else jnp.concatenate(pieces, axis=0)
        n = rows.shape[0]
        sq = rows * rows
        sq = sum(sq[:, 128 * i : 128 * i + 128] for i in range(width // 128))
        cnb[at : at + n, :] = jnp.broadcast_to(jnp.sum(sq, axis=1, keepdims=True), (n, 128))
        hi = rows.astype(BF16)
        c3[at : at + n, 0:width] = hi
        c3[at : at + n, width : 2 * width] = hi
        c3[at : at + n, 2 * width : 3 * width] = (rows - hi.astype(F32)).astype(BF16)

    def nearest(at, n):
        d = jnp.dot(c3[at : at + n, :], p3[...], preferred_element_type=F32)
        d = d + jnp.concatenate([cnb[at : at + n, :]] * (npts // 128), axis=1)
        acc[...] = jnp.minimum(acc[...], jnp.min(d.reshape(n // 8, 8, npts), axis=0))

    def others(pos):
        return ga[pos].reshape((NX - 1) * RA, width)

    fill(208, [own[0], own[0, 0:16]])
    for copy in own_a:
        copy.wait_recv()
    all_dn(0).start()
    all_up(0).start()

    def tick(t, _):
        for i in range(SPLIT):
            own_up(i, t - 1).wait_recv()

            @pl.when(t < HALF)
            def _():
                own_up(i, t).start()
                own_dn(i, t - 1).wait_recv()

            @pl.when(t < HALF - 1)
            def _():
                own_dn(i, t).start()

        @pl.when(t < HALF)
        def _():
            xr(t).start()
            xl(t).start()
            fill(0, [own[2 * t - 1], own[2 * t]])

        @pl.when(t == HALF)
        def _():
            for copy in last_b:
                copy.start()
            fill(0, [own[far], own[far]])

        @pl.when(t == 1)
        def _():
            for copy in own_b:
                copy.wait_recv()
            fill(64, [gb[0, 0], gb[1, 0], gb[2, 0], others(0)])

        @pl.when(t >= 3)
        def _():
            fill(64, [gb[2, 2 * t - 5], gb[2, 2 * t - 4], gb[0, 2 * t - 5], gb[0, 2 * t - 4]])

        nearest(0, 160)

        @pl.when(t == HALF)
        def _():
            relay(t - 1)

        all_dn(t - 1).wait_recv()

        @pl.when(t < HALF)
        def _():
            all_dn(t).start()
            all_up(t - 1).wait_recv()

        @pl.when(t < HALF - 1)
        def _():
            all_up(t).start()

        @pl.when(t < HALF)
        def _():
            fill(160, [others(2 * t - 1), others(2 * t)])

        @pl.when(t == HALF)
        def _():
            fill(160, [others(2 * HALF), others(2 * HALF)])

        @pl.when(t >= 4)
        def _():
            rel_r(t - 3).wait_recv()
            rel_l(t - 3).wait_recv()
            fill(208, [gb[1, 2 * t - 7], gb[1, 2 * t - 6]])

        nearest(160, 96)

        @pl.when((t >= 2) & (t < HALF))
        def _():
            relay(t - 1)

        for i in range(SPLIT):
            own_up(i, t - 1).wait_send()
        all_dn(t - 1).wait_send()

        @pl.when(t < HALF)
        def _():
            for i in range(SPLIT):
                own_dn(i, t - 1).wait_send()
            all_up(t - 1).wait_send()

        @pl.when(t >= 2)
        def _():
            xr(t - 1).wait_send()
            xl(t - 1).wait_send()

        @pl.when(t >= 3)
        def _():
            rel_r(t - 2).wait_send()
            rel_l(t - 2).wait_send()

        return 0

    def relay(t):
        xr(t).wait_recv()
        xl(t).wait_recv()
        rel_r(t).start()
        rel_l(t).start()

    lax.fori_loop(1, HALF + 1, tick, 0)

    fill(0, [gb[2, 13], gb[2, 14], gb[0, 13], gb[0, 14]])
    rel_r(HALF - 2).wait_recv()
    rel_l(HALF - 2).wait_recv()
    fill(96, [gb[1, 11], gb[1, 12]])
    nearest(0, 144)
    for copy in own_a + own_b:
        copy.wait_send()
    for copy in last_b:
        copy.wait_recv()
    rel_r(HALF - 1).wait_recv()
    rel_l(HALF - 1).wait_recv()
    fill(0, [gb[1, 13], gb[1, 14], gb[0, 15], gb[1, 15], gb[2, 15], gb[2, 15, 0:8]])
    nearest(0, 128)
    rel_r(HALF - 1).wait_send()
    rel_l(HALF - 1).wait_send()

    low = jnp.min(acc[...], axis=0, keepdims=True)
    low = (low + pn[...]) / width
    for i in range(npts // 128):
        mins[0, i : i + 1, :] = low[:, 128 * i : 128 * i + 128]
    swaps = [remote(mins.at[0], mins.at[j], scm.at[j], rcm.at[j], mate(j)) for j in range(1, NC)]
    for copy in swaps:
        copy.start()
    for copy in last_b:
        copy.wait_send()
    new = jnp.minimum(prior_ref[...], mins[0])
    for copy in swaps:
        copy.wait_recv()
    for j in range(1, NC):
        new = jnp.minimum(new, mins[j])
    out_ref[...] = new

    sx[x] = jnp.sum(new, axis=0, keepdims=True)
    sums = [
        remote(sx.at[x], sx.at[x], scx.at[d], rcx.at[d], peer(0, d)) for d in range(1, NX)
    ]
    for copy in sums:
        copy.start()
    for copy in swaps:
        copy.wait_send()
    for d in range(1, NX):
        src = lax.rem(x - d + NX, NX)
        remote(sx.at[x], sx.at[src], scx.at[d], rcx.at[d], peer(0, d)).wait_recv()
    sz[z] = (sx[0] + sx[1]) + (sx[2] + sx[3])
    sumz = [
        remote(sz.at[z], sz.at[z], scz.at[d], rcz.at[d], peer(d, 0)) for d in range(1, NZ)
    ]
    for copy in sumz:
        copy.start()
    for copy in sums:
        copy.wait_send()
    for d in range(1, NZ):
        src = lax.rem(z - d + NZ, NZ)
        remote(sz.at[z], sz.at[src], scz.at[d], rcz.at[d], peer(d, 0)).wait_recv()
    total = sz[0]
    for i in range(1, NZ):
        total = total + sz[i]
    cost_ref[...] = jnp.broadcast_to(
        jnp.sum(total, axis=1, keepdims=True) / (npts * NZ * NX), cost_ref.shape
    )
    for copy in sumz:
        copy.wait_send()


def hbm(array):
    return pltpu.with_memory_space_constraint(array, pltpu.HBM)


def local(points, prior_min, cand_slots):
    npts, width = points.shape
    vmem = pl.BlockSpec(memory_space=pltpu.VMEM)
    dma = pltpu.SemaphoreType.DMA
    new, cost = pl.pallas_call(
        kernel,
        out_shape=(
            jax.ShapeDtypeStruct((npts // 128, 128), F32),
            jax.ShapeDtypeStruct((1, 128), F32),
        ),
        in_specs=[pl.BlockSpec(memory_space=pltpu.HBM)] * 3,
        out_specs=(vmem, vmem),
        scratch_shapes=[
            pltpu.SMEM((RA + RB,), jnp.int32),
            pltpu.VMEM((npts // 128, 128), F32),
            pltpu.VMEM((npts, width), F32),
            pltpu.VMEM((3 * width, npts), BF16),
            pltpu.VMEM((1, npts), F32),
            pltpu.VMEM((NZ, RA + RB, width), F32),
            pltpu.VMEM((NZ + 1, NX - 1, RA, width), F32),
            pltpu.VMEM((NX - 1, NZ, RB, width), F32),
            pltpu.VMEM((256, 3 * width), BF16),
            pltpu.VMEM((256, 128), F32),
            pltpu.VMEM((8, npts), F32),
            pltpu.VMEM((NC, npts // 128, 128), F32),
            pltpu.VMEM((NX, 1, 128), F32),
            pltpu.VMEM((NZ, 1, 128), F32),
            dma((6,)), dma((10, 2)),
            dma((SPLIT, 2, HALF + 1)), dma((2, HALF + 1)), dma((2, HALF + 1)), dma((2, HALF + 1)),
            dma((3,)), dma((6,)), dma((9,)),
            dma((NC,)), dma((NC,)), dma((NX,)), dma((NX,)), dma((NZ,)), dma((NZ,)),
        ],
        compiler_params=pltpu.CompilerParams(
            collective_id=0, has_side_effects=True, vmem_limit_bytes=48 << 20
        ),
    )(hbm(points), hbm(prior_min.reshape(npts // 128, 128)), hbm(cand_slots.reshape(-1)))
    return new.reshape(-1), cost[0, 0]


def solution(mesh):
    placed = (P("pts", None), P("pts"), P("pts", "cand", None))
    return jax.shard_map(
        local, mesh=mesh, in_specs=placed, out_specs=(P("pts"), P()), check_vma=False
    )
```

```python
import functools

import jax
import jax.numpy as jnp
from jax import lax
from jax.experimental import pallas as pl
from jax.experimental.pallas import tpu as pltpu
from jax.sharding import PartitionSpec as P

MESH = pl.DeviceIdType.MESH
NX, NZ, NC = 4, 16, 8
HALF = NZ // 2
RA, RB = 8, 24
SPLIT = 2
F32, BF16 = jnp.float32, jnp.bfloat16


def when(condition):
    return lambda body: body() if condition else None


def kernel(
    pts_hbm, prior_hbm, slots_hbm, out_ref, cost_ref,
    slots_ref, prior_ref, pf, p3, pn, own, ga, gb, c3, cnb, acc, mins, sz,
    load_sem, ssem, rown, rall, rx, rr, rax, rbx, s0, scm, rcm, scz, rcz,
):
    p, c = lax.axis_index("pts"), lax.axis_index("cand")
    z, x = p // NX, p % NX
    npts, width = pf.shape
    quarter = npts // 4

    def peer(dz, dx):
        return (lax.rem(z + dz + NZ, NZ) * NX + lax.rem(x + dx + NX, NX), c)

    def mate(j):
        return (p, lax.rem(c + j, NC))

    def remote(src, dst, send, recv, where):
        return pltpu.make_async_remote_copy(
            src_ref=src, dst_ref=dst, send_sem=send, recv_sem=recv,
            device_id=where, device_id_type=MESH,
        )

    zu, zd, xu, xd = peer(-1, 0), peer(1, 0), peer(0, 1), peer(0, -1)
    loads = []
    for q in range(4):
        rows = pl.ds(q * quarter, quarter)
        load = pltpu.make_async_copy(pts_hbm.at[rows], pf.at[rows], load_sem.at[q])
        load.start()
        loads.append(load)

    barrier = pltpu.get_barrier_semaphore()
    near = [peer(1, 0), peer(-1, 0), peer(0, 1), peer(0, -1), peer(0, 2)]
    near += [mate(j) for j in range(1, NC)]
    for who in near:
        pl.semaphore_signal(barrier, inc=1, device_id=who, device_id_type=MESH)
    slots_copy = pltpu.make_async_copy(slots_hbm, slots_ref, load_sem.at[4])
    slots_copy.start()
    prior_copy = pltpu.make_async_copy(prior_hbm, prior_ref, load_sem.at[5])
    prior_copy.start()
    acc[...] = jnp.full(acc.shape, 3e38, F32)
    slots_copy.wait()
    prior_copy.wait()
    for load in loads:
        load.wait()

    first = slots_ref[0]
    for i in range(RA + RB):
        slot = slots_ref[i]
        own[0, i : i + 1, :] = pf[pl.ds(jnp.where(slot >= 0, slot, first), 1), :]

    pl.semaphore_wait(barrier, len(near))

    def up(t):
        return max(2 * t - 1, 0)

    def sent(kind, t):
        return ssem.at[kind, t % 2]

    parts = [pl.ds(i * (RA + RB) // SPLIT, (RA + RB) // SPLIT) for i in range(SPLIT)]

    def own_up(i, t):
        src, dst = own.at[up(t), parts[i]], own.at[2 * t + 1, parts[i]]
        return remote(src, dst, sent(i, t), rown.at[i, 0, t + 1], zu)

    def own_dn(i, t):
        src, dst = own.at[2 * t, parts[i]], own.at[2 * t + 2, parts[i]]
        return remote(src, dst, sent(2 + i, t), rown.at[i, 1, t + 1], zd)

    def all_up(t):
        return remote(ga.at[up(t)], ga.at[2 * t + 1], sent(4, t), rall.at[0, t + 1], zu)

    def all_dn(t):
        return remote(ga.at[2 * t], ga.at[2 * t + 2], sent(5, t), rall.at[1, t + 1], zd)

    def xr(t):
        two = pl.ds(2 * t - 1, 2)
        src = own.at[two, pl.ds(RA, RB)]
        return remote(src, gb.at[2, two], sent(6, t), rx.at[0, t], xu)

    def xl(t):
        two = pl.ds(2 * t - 1, 2)
        src = own.at[two, pl.ds(RA, RB)]
        return remote(src, gb.at[0, two], sent(7, t), rx.at[1, t], xd)

    def rel_r(t):
        at = 2 * t - 1
        return remote(gb.at[2, at], gb.at[1, at], sent(8, t), rr.at[0, t], xu)

    def rel_l(t):
        return remote(gb.at[0, 2 * t], gb.at[1, 2 * t], sent(9, t), rr.at[1, t], xd)

    around = (3, 1, 2)
    own_a = [
        remote(own.at[0, pl.ds(0, RA)], ga.at[0, d - 1], s0.at[i], rax.at[i], peer(0, -d))
        for i, d in enumerate(around)
    ]
    own_b = [
        remote(own.at[0, pl.ds(RA, RB)], gb.at[d - 1, 0], s0.at[3 + i], rbx.at[i], peer(0, -d))
        for i, d in enumerate(around)
    ]
    far = 2 * HALF - 1
    last_b = [
        remote(own.at[far, pl.ds(RA, RB)], gb.at[d - 1, far], s0.at[6 + i], rbx.at[3 + i], peer(0, -d))
        for i, d in enumerate(around)
    ]

    for copy in own_a:
        copy.start()
    for i in range(SPLIT):
        own_up(i, 0).start()
        own_dn(i, 0).start()
    for copy in own_b:
        copy.start()

    for q in range(npts // 256):
        cols = pl.ds(q * 256, 256)
        t = pf[cols, :].T
        pn[:, cols] = jnp.sum(t * t, axis=0, keepdims=True)
        t = t * -2.0
        hi = t.astype(BF16)
        lo = (t - hi.astype(F32)).astype(BF16)
        p3[0:width, cols] = hi
        p3[width : 2 * width, cols] = lo
        p3[2 * width : 3 * width, cols] = hi

    def fill(at, pieces):
        rows = pieces[0] if len(pieces) == 1 else jnp.concatenate(pieces, axis=0)
        n = rows.shape[0]
        sq = rows * rows
        sq = sum(sq[:, 128 * i : 128 * i + 128] for i in range(width // 128))
        cnb[at : at + n, :] = jnp.broadcast_to(jnp.sum(sq, axis=1, keepdims=True), (n, 128))
        hi = rows.astype(BF16)
        c3[at : at + n, 0:width] = hi
        c3[at : at + n, width : 2 * width] = hi
        c3[at : at + n, 2 * width : 3 * width] = (rows - hi.astype(F32)).astype(BF16)

    def nearest(at, n):
        d = jnp.dot(c3[at : at + n, :], p3[...], preferred_element_type=F32)
        d = d + jnp.concatenate([cnb[at : at + n, :]] * (npts // 128), axis=1)
        acc[...] = jnp.minimum(acc[...], jnp.min(d.reshape(n // 8, 8, npts), axis=0))

    def others(pos):
        return ga[pos].reshape((NX - 1) * RA, width)

    fill(208, [own[0], own[0, 0:16]])
    for copy in own_a:
        copy.wait_recv()
    all_dn(0).start()
    all_up(0).start()

    def tick(t, _):
        for i in range(SPLIT):
            own_up(i, t - 1).wait_recv()

            @when(t < HALF)
            def _():
                own_up(i, t).start()
                own_dn(i, t - 1).wait_recv()

            @when(t < HALF - 1)
            def _():
                own_dn(i, t).start()

        @when(t < HALF)
        def _():
            xr(t).start()
            xl(t).start()
            fill(0, [own[2 * t - 1], own[2 * t]])

        @when(t == HALF)
        def _():
            for copy in last_b:
                copy.start()
            fill(0, [own[far], own[far]])

        @when(t == 1)
        def _():
            for copy in own_b:
                copy.wait_recv()
            fill(64, [gb[0, 0], gb[1, 0], gb[2, 0], others(0)])

        @when(t >= 3)
        def _():
            fill(64, [gb[2, 2 * t - 5], gb[2, 2 * t - 4], gb[0, 2 * t - 5], gb[0, 2 * t - 4]])

        nearest(0, 160)

        @when(t == HALF)
        def _():
            relay(t - 1)

        all_dn(t - 1).wait_recv()

        @when(t < HALF)
        def _():
            all_dn(t).start()
            all_up(t - 1).wait_recv()

        @when(t < HALF - 1)
        def _():
            all_up(t).start()

        @when(t < HALF)
        def _():
            fill(160, [others(2 * t - 1), others(2 * t)])

        @when(t == HALF)
        def _():
            fill(160, [others(2 * HALF), others(2 * HALF)])

        @when(t >= 4)
        def _():
            rel_r(t - 3).wait_recv()
            rel_l(t - 3).wait_recv()
            fill(208, [gb[1, 2 * t - 7], gb[1, 2 * t - 6]])

        nearest(160, 96)

        @when(t >= 2 and t < HALF)
        def _():
            relay(t - 1)

        for i in range(SPLIT):
            own_up(i, t - 1).wait_send()
        all_dn(t - 1).wait_send()

        @when(t < HALF)
        def _():
            for i in range(SPLIT):
                own_dn(i, t - 1).wait_send()
            all_up(t - 1).wait_send()

        @when(t >= 2)
        def _():
            xr(t - 1).wait_send()
            xl(t - 1).wait_send()

        @when(t >= 3)
        def _():
            rel_r(t - 2).wait_send()
            rel_l(t - 2).wait_send()

        return 0

    def relay(t):
        xr(t).wait_recv()
        xl(t).wait_recv()
        rel_r(t).start()
        rel_l(t).start()

    for t in range(1, HALF + 1):
        tick(t, 0)

    fill(0, [gb[2, 13], gb[2, 14], gb[0, 13], gb[0, 14]])
    rel_r(HALF - 2).wait_recv()
    rel_l(HALF - 2).wait_recv()
    fill(96, [gb[1, 11], gb[1, 12]])
    nearest(0, 144)
    for copy in own_a + own_b:
        copy.wait_send()
    for copy in last_b:
        copy.wait_recv()
    rel_r(HALF - 1).wait_recv()
    rel_l(HALF - 1).wait_recv()
    fill(0, [gb[1, 13], gb[1, 14], gb[0, 15], gb[1, 15], gb[2, 15], gb[2, 15, 0:8]])
    nearest(0, 128)
    rel_r(HALF - 1).wait_send()
    rel_l(HALF - 1).wait_send()

    low = jnp.min(acc[...], axis=0, keepdims=True)
    low = (low + pn[...]) / width
    for i in range(npts // 128):
        mins[0, i : i + 1, :] = low[:, 128 * i : 128 * i + 128]
    swaps = [remote(mins.at[0], mins.at[j], scm.at[j], rcm.at[j], mate(j)) for j in range(1, NC)]
    for copy in swaps:
        copy.start()
    for copy in last_b:
        copy.wait_send()
    new = jnp.minimum(prior_ref[...], mins[0])
    for copy in swaps:
        copy.wait_recv()
    for j in range(1, NC):
        new = jnp.minimum(new, mins[j])
    out_ref[...] = new

    sz[p] = jnp.sum(new, axis=0, keepdims=True)
    order = sorted(range(1, NZ * NX), key=lambda d: -(min(d // NX, NZ - d // NX) + min(d % NX, NX - d % NX)))

    def total_at(i, slot):
        d = order[i]
        return remote(sz.at[p], sz.at[slot], scz.at[i], rcz.at[i], peer(d // NX, d % NX))

    sums = [total_at(i, p) for i in range(NZ * NX - 1)]
    for copy in sums:
        copy.start()
    for copy in swaps:
        copy.wait_send()
    for i, d in enumerate(order):
        src = lax.rem(z - d // NX + NZ, NZ) * NX + lax.rem(x - d % NX + NX, NX)
        total_at(i, src).wait_recv()
    total = jnp.sum(sz[...], axis=0)
    cost_ref[...] = jnp.broadcast_to(
        jnp.sum(total, axis=1, keepdims=True) / (npts * NZ * NX), cost_ref.shape
    )
    for copy in sums:
        copy.wait_send()


def hbm(array):
    return pltpu.with_memory_space_constraint(array, pltpu.HBM)


def local(points, prior_min, cand_slots):
    npts, width = points.shape
    vmem = pl.BlockSpec(memory_space=pltpu.VMEM)
    dma = pltpu.SemaphoreType.DMA
    new, cost = pl.pallas_call(
        kernel,
        out_shape=(
            jax.ShapeDtypeStruct((npts // 128, 128), F32),
            jax.ShapeDtypeStruct((1, 128), F32),
        ),
        in_specs=[pl.BlockSpec(memory_space=pltpu.HBM)] * 3,
        out_specs=(vmem, vmem),
        scratch_shapes=[
            pltpu.SMEM((RA + RB,), jnp.int32),
            pltpu.VMEM((npts // 128, 128), F32),
            pltpu.VMEM((npts, width), F32),
            pltpu.VMEM((3 * width, npts), BF16),
            pltpu.VMEM((1, npts), F32),
            pltpu.VMEM((NZ, RA + RB, width), F32),
            pltpu.VMEM((NZ + 1, NX - 1, RA, width), F32),
            pltpu.VMEM((NX - 1, NZ, RB, width), F32),
            pltpu.VMEM((256, 3 * width), BF16),
            pltpu.VMEM((256, 128), F32),
            pltpu.VMEM((8, npts), F32),
            pltpu.VMEM((NC, npts // 128, 128), F32),
            pltpu.VMEM((NZ * NX, 1, 128), F32),
            dma((6,)), dma((10, 2)),
            dma((SPLIT, 2, HALF + 1)), dma((2, HALF + 1)), dma((2, HALF + 1)), dma((2, HALF + 1)),
            dma((3,)), dma((6,)), dma((9,)),
            dma((NC,)), dma((NC,)), dma((NZ * NX,)), dma((NZ * NX,)),
        ],
        compiler_params=pltpu.CompilerParams(
            collective_id=0, has_side_effects=True, vmem_limit_bytes=48 << 20
        ),
    )(hbm(points), hbm(prior_min.reshape(npts // 128, 128)), hbm(cand_slots.reshape(-1)))
    return new.reshape(-1), cost[0, 0]


def solution(mesh):
    placed = (P("pts", None), P("pts"), P("pts", "cand", None))
    return jax.shard_map(
        local, mesh=mesh, in_specs=placed, out_specs=(P("pts"), P()), check_vma=False
    )
```

```python
import functools

import jax
import jax.numpy as jnp
from jax import lax
from jax.experimental import pallas as pl
from jax.experimental.pallas import tpu as pltpu
from jax.sharding import PartitionSpec as P

MESH = pl.DeviceIdType.MESH
NX, NZ, NC = 4, 16, 8
HALF = NZ // 2
RA, RB = 8, 24
SPLIT = 2
F32, BF16 = jnp.float32, jnp.bfloat16


def when(condition):
    return lambda body: body() if condition else None


def kernel(
    pts_hbm, prior_hbm, slots_hbm, out_ref, cost_ref,
    slots_ref, prior_ref, pf, p3, pn, own, ga, gb, c3, cnb, acc, mins, sz,
    load_sem, ssem, rown, rall, rx, rr, rax, rbx, s0, scm, rcm, scz, rcz,
):
    p, c = lax.axis_index("pts"), lax.axis_index("cand")
    z, x = p // NX, p % NX
    npts, width = pf.shape
    quarter = npts // 4

    def peer(dz, dx):
        return (lax.rem(z + dz + NZ, NZ) * NX + lax.rem(x + dx + NX, NX), c)

    def mate(j):
        return (p, lax.rem(c + j, NC))

    def remote(src, dst, send, recv, where):
        return pltpu.make_async_remote_copy(
            src_ref=src, dst_ref=dst, send_sem=send, recv_sem=recv,
            device_id=where, device_id_type=MESH,
        )

    zu, zd, xu, xd = peer(-1, 0), peer(1, 0), peer(0, 1), peer(0, -1)
    loads = []
    for q in range(4):
        rows = pl.ds(q * quarter, quarter)
        load = pltpu.make_async_copy(pts_hbm.at[rows], pf.at[rows], load_sem.at[q])
        load.start()
        loads.append(load)

    barrier = pltpu.get_barrier_semaphore()
    near = [peer(1, 0), peer(-1, 0), peer(0, 1), peer(0, -1), peer(0, 2)]
    near += [mate(j) for j in range(1, NC)]
    for who in near:
        pl.semaphore_signal(barrier, inc=1, device_id=who, device_id_type=MESH)
    slots_copy = pltpu.make_async_copy(slots_hbm, slots_ref, load_sem.at[4])
    slots_copy.start()
    prior_copy = pltpu.make_async_copy(prior_hbm, prior_ref, load_sem.at[5])
    prior_copy.start()
    acc[...] = jnp.full(acc.shape, 3e38, F32)
    slots_copy.wait()
    prior_copy.wait()
    for load in loads:
        load.wait()

    first = slots_ref[0]
    for i in range(RA + RB):
        slot = slots_ref[i]
        own[0, i : i + 1, :] = pf[pl.ds(jnp.where(slot >= 0, slot, first), 1), :]

    pl.semaphore_wait(barrier, len(near))

    def up(t):
        return max(2 * t - 1, 0)

    def sent(kind, t):
        return ssem.at[kind, t % 2]

    parts = [pl.ds(i * (RA + RB) // SPLIT, (RA + RB) // SPLIT) for i in range(SPLIT)]

    def own_up(i, t):
        src, dst = own.at[up(t), parts[i]], own.at[2 * t + 1, parts[i]]
        return remote(src, dst, sent(i, t), rown.at[i, 0, t + 1], zu)

    def own_dn(i, t):
        src, dst = own.at[2 * t, parts[i]], own.at[2 * t + 2, parts[i]]
        return remote(src, dst, sent(2 + i, t), rown.at[i, 1, t + 1], zd)

    def all_up(t):
        return remote(ga.at[up(t)], ga.at[2 * t + 1], sent(4, t), rall.at[0, t + 1], zu)

    def all_dn(t):
        return remote(ga.at[2 * t], ga.at[2 * t + 2], sent(5, t), rall.at[1, t + 1], zd)

    def xr(t):
        two = pl.ds(2 * t - 1, 2)
        src = own.at[two, pl.ds(RA, RB)]
        return remote(src, gb.at[2, two], sent(6, t), rx.at[0, t], xu)

    def xl(t):
        two = pl.ds(2 * t - 1, 2)
        src = own.at[two, pl.ds(RA, RB)]
        return remote(src, gb.at[0, two], sent(7, t), rx.at[1, t], xd)

    def rel_r(t):
        at = 2 * t - 1
        return remote(gb.at[2, at], gb.at[1, at], sent(8, t), rr.at[0, t], xu)

    def rel_l(t):
        return remote(gb.at[0, 2 * t], gb.at[1, 2 * t], sent(9, t), rr.at[1, t], xd)

    around = (3, 1, 2)
    own_a = [
        remote(own.at[0, pl.ds(0, RA)], ga.at[0, d - 1], s0.at[i], rax.at[i], peer(0, -d))
        for i, d in enumerate(around)
    ]
    own_b = [
        remote(own.at[0, pl.ds(RA, RB)], gb.at[d - 1, 0], s0.at[3 + i], rbx.at[i], peer(0, -d))
        for i, d in enumerate(around)
    ]
    far = 2 * HALF - 1
    last_b = [
        remote(own.at[far, pl.ds(RA, RB)], gb.at[d - 1, far], s0.at[6 + i], rbx.at[3 + i], peer(0, -d))
        for i, d in enumerate(around)
    ]

    for copy in own_a:
        copy.start()
    for i in range(SPLIT):
        own_up(i, 0).start()
        own_dn(i, 0).start()
    for copy in own_b:
        copy.start()

    for q in range(npts // 256):
        cols = pl.ds(q * 256, 256)
        t = pf[cols, :].T
        pn[:, cols] = jnp.sum(t * t, axis=0, keepdims=True)
        t = t * -2.0
        hi = t.astype(BF16)
        lo = (t - hi.astype(F32)).astype(BF16)
        p3[0:width, cols] = hi
        p3[width : 2 * width, cols] = lo
        p3[2 * width : 3 * width, cols] = hi

    def fill(at, pieces):
        rows = pieces[0] if len(pieces) == 1 else jnp.concatenate(pieces, axis=0)
        n = rows.shape[0]
        sq = rows * rows
        sq = sum(sq[:, 128 * i : 128 * i + 128] for i in range(width // 128))
        cnb[at : at + n, :] = jnp.broadcast_to(jnp.sum(sq, axis=1, keepdims=True), (n, 128))
        hi = rows.astype(BF16)
        c3[at : at + n, 0:width] = hi
        c3[at : at + n, width : 2 * width] = hi
        c3[at : at + n, 2 * width : 3 * width] = (rows - hi.astype(F32)).astype(BF16)

    def nearest(at, n):
        d = jnp.dot(c3[at : at + n, :], p3[...], preferred_element_type=F32)
        d = d + jnp.concatenate([cnb[at : at + n, :]] * (npts // 128), axis=1)
        acc[...] = jnp.minimum(acc[...], jnp.min(d.reshape(n // 8, 8, npts), axis=0))

    def others(pos):
        return ga[pos].reshape((NX - 1) * RA, width)

    fill(208, [own[0], own[0, 0:16]])
    for copy in own_a:
        copy.wait_recv()
    all_dn(0).start()
    all_up(0).start()

    def tick(t, _):
        for i in range(SPLIT):
            own_up(i, t - 1).wait_recv()

            @when(t < HALF)
            def _():
                own_up(i, t).start()
                own_dn(i, t - 1).wait_recv()

            @when(t < HALF - 1)
            def _():
                own_dn(i, t).start()

        @when(t < HALF)
        def _():
            xr(t).start()
            xl(t).start()
            fill(0, [own[2 * t - 1], own[2 * t]])

        @when(t == HALF)
        def _():
            for copy in last_b:
                copy.start()
            fill(0, [own[far], own[far]])

        @when(t == 1)
        def _():
            for copy in own_b:
                copy.wait_recv()
            fill(64, [gb[0, 0], gb[1, 0], gb[2, 0], others(0)])

        @when(t >= 3)
        def _():
            fill(64, [gb[2, 2 * t - 5], gb[2, 2 * t - 4], gb[0, 2 * t - 5], gb[0, 2 * t - 4]])

        nearest(0, 160)

        @when(t == HALF)
        def _():
            relay(t - 1)

        all_dn(t - 1).wait_recv()

        @when(t < HALF)
        def _():
            all_dn(t).start()
            all_up(t - 1).wait_recv()

        @when(t < HALF - 1)
        def _():
            all_up(t).start()

        @when(t < HALF)
        def _():
            fill(160, [others(2 * t - 1), others(2 * t)])

        @when(t == HALF)
        def _():
            fill(160, [others(2 * HALF), others(2 * HALF)])

        @when(t >= 4)
        def _():
            rel_r(t - 3).wait_recv()
            rel_l(t - 3).wait_recv()
            fill(208, [gb[1, 2 * t - 7], gb[1, 2 * t - 6]])

        nearest(160, 96)

        @when(t >= 2 and t < HALF)
        def _():
            relay(t - 1)

        for i in range(SPLIT):
            own_up(i, t - 1).wait_send()
        all_dn(t - 1).wait_send()

        @when(t < HALF)
        def _():
            for i in range(SPLIT):
                own_dn(i, t - 1).wait_send()
            all_up(t - 1).wait_send()

        @when(t >= 2)
        def _():
            xr(t - 1).wait_send()
            xl(t - 1).wait_send()

        @when(t >= 3)
        def _():
            rel_r(t - 2).wait_send()
            rel_l(t - 2).wait_send()

        return 0

    def relay(t):
        xr(t).wait_recv()
        xl(t).wait_recv()
        rel_r(t).start()
        rel_l(t).start()

    for t in range(1, HALF + 1):
        tick(t, 0)

    fill(0, [gb[2, 13], gb[2, 14], gb[0, 13], gb[0, 14]])
    rel_r(HALF - 2).wait_recv()
    rel_l(HALF - 2).wait_recv()
    fill(96, [gb[1, 11], gb[1, 12]])
    nearest(0, 144)
    for copy in own_a + own_b:
        copy.wait_send()
    for copy in last_b:
        copy.wait_recv()
    rel_r(HALF - 1).wait_recv()
    rel_l(HALF - 1).wait_recv()
    fill(0, [gb[1, 13], gb[1, 14], gb[0, 15], gb[1, 15], gb[2, 15], gb[2, 15, 0:8]])
    nearest(0, 128)
    rel_r(HALF - 1).wait_send()
    rel_l(HALF - 1).wait_send()

    low = jnp.min(acc[...], axis=0, keepdims=True)
    low = (low + pn[...]) / width
    for i in range(npts // 128):
        mins[0, i : i + 1, :] = low[:, 128 * i : 128 * i + 128]
    swaps = [remote(mins.at[0], mins.at[j], scm.at[j], rcm.at[j], mate(j)) for j in range(1, NC)]
    for copy in swaps:
        copy.start()
    for copy in last_b:
        copy.wait_send()
    new = jnp.minimum(prior_ref[...], mins[0])
    for copy in swaps:
        copy.wait_recv()
    for j in range(1, NC):
        new = jnp.minimum(new, mins[j])
    out_ref[...] = new

    sz[p] = jnp.sum(new, axis=0, keepdims=True)
    order = sorted(range(1, NZ * NX), key=lambda d: -(min(d // NX, NZ - d // NX) + min(d % NX, NX - d % NX)))

    def total_at(i, slot):
        d = order[i]
        return remote(sz.at[p], sz.at[slot], scz.at[i], rcz.at[i], peer(d // NX, d % NX))

    sums = [total_at(i, p) for i in range(NZ * NX - 1)]
    for copy in sums:
        copy.start()
    for copy in swaps:
        copy.wait_send()
    for copy in sums:
        copy.wait_send()
    for i, d in reversed(list(enumerate(order))):
        src = lax.rem(z - d // NX + NZ, NZ) * NX + lax.rem(x - d % NX + NX, NX)
        total_at(i, src).wait_recv()
    total = jnp.sum(sz[...], axis=0)
    cost_ref[...] = jnp.broadcast_to(
        jnp.sum(total, axis=1, keepdims=True) / (npts * NZ * NX), cost_ref.shape
    )


def hbm(array):
    return pltpu.with_memory_space_constraint(array, pltpu.HBM)


def local(points, prior_min, cand_slots):
    npts, width = points.shape
    vmem = pl.BlockSpec(memory_space=pltpu.VMEM)
    dma = pltpu.SemaphoreType.DMA
    new, cost = pl.pallas_call(
        kernel,
        out_shape=(
            jax.ShapeDtypeStruct((npts // 128, 128), F32),
            jax.ShapeDtypeStruct((1, 128), F32),
        ),
        in_specs=[pl.BlockSpec(memory_space=pltpu.HBM)] * 3,
        out_specs=(vmem, vmem),
        scratch_shapes=[
            pltpu.SMEM((RA + RB,), jnp.int32),
            pltpu.VMEM((npts // 128, 128), F32),
            pltpu.VMEM((npts, width), F32),
            pltpu.VMEM((3 * width, npts), BF16),
            pltpu.VMEM((1, npts), F32),
            pltpu.VMEM((NZ, RA + RB, width), F32),
            pltpu.VMEM((NZ + 1, NX - 1, RA, width), F32),
            pltpu.VMEM((NX - 1, NZ, RB, width), F32),
            pltpu.VMEM((256, 3 * width), BF16),
            pltpu.VMEM((256, 128), F32),
            pltpu.VMEM((8, npts), F32),
            pltpu.VMEM((NC, npts // 128, 128), F32),
            pltpu.VMEM((NZ * NX, 1, 128), F32),
            dma((6,)), dma((10, 2)),
            dma((SPLIT, 2, HALF + 1)), dma((2, HALF + 1)), dma((2, HALF + 1)), dma((2, HALF + 1)),
            dma((3,)), dma((6,)), dma((9,)),
            dma((NC,)), dma((NC,)), dma((NZ * NX,)), dma((NZ * NX,)),
        ],
        compiler_params=pltpu.CompilerParams(
            collective_id=0, has_side_effects=True, vmem_limit_bytes=48 << 20
        ),
    )(hbm(points), hbm(prior_min.reshape(npts // 128, 128)), hbm(cand_slots.reshape(-1)))
    return new.reshape(-1), cost[0, 0]


def solution(mesh):
    placed = (P("pts", None), P("pts"), P("pts", "cand", None))
    return jax.shard_map(
        local, mesh=mesh, in_specs=placed, out_specs=(P("pts"), P()), check_vma=False
    )
```

```python
import functools

import jax
import jax.numpy as jnp
from jax import lax
from jax.experimental import pallas as pl
from jax.experimental.pallas import tpu as pltpu
from jax.sharding import PartitionSpec as P

MESH = pl.DeviceIdType.MESH
NX, NZ, NC = 4, 16, 8
HALF = NZ // 2
RA, RB = 8, 24
SPLIT = 2
F32, BF16 = jnp.float32, jnp.bfloat16


def when(condition):
    return lambda body: body() if condition else None


def kernel(
    pts_hbm, prior_hbm, slots_hbm, out_ref, cost_ref,
    slots_ref, prior_ref, pf, p3, pn, own, ga, gb, c3, cnb, acc, mins, sz,
    load_sem, ssem, rown, rall, rx, rr, rax, rbx, s0, scm, rcm, scz, rcz,
):
    p, c = lax.axis_index("pts"), lax.axis_index("cand")
    z, x = p // NX, p % NX
    npts, width = pf.shape
    quarter = npts // 4

    def peer(dz, dx):
        return (lax.rem(z + dz + NZ, NZ) * NX + lax.rem(x + dx + NX, NX), c)

    def mate(j):
        return (p, lax.rem(c + j, NC))

    def remote(src, dst, send, recv, where):
        return pltpu.make_async_remote_copy(
            src_ref=src, dst_ref=dst, send_sem=send, recv_sem=recv,
            device_id=where, device_id_type=MESH,
        )

    zu, zd, xu, xd = peer(-1, 0), peer(1, 0), peer(0, 1), peer(0, -1)
    barrier = pltpu.get_barrier_semaphore()
    near = [peer(1, 0), peer(-1, 0), peer(0, 1), peer(0, -1), peer(0, 2)]
    near += [mate(j) for j in range(1, NC)]
    for who in near:
        pl.semaphore_signal(barrier, inc=1, device_id=who, device_id_type=MESH)
    loads = []
    for q in range(4):
        rows = pl.ds(q * quarter, quarter)
        load = pltpu.make_async_copy(pts_hbm.at[rows], pf.at[rows], load_sem.at[q])
        load.start()
        loads.append(load)
    slots_copy = pltpu.make_async_copy(slots_hbm, slots_ref, load_sem.at[4])
    slots_copy.start()
    prior_copy = pltpu.make_async_copy(prior_hbm, prior_ref, load_sem.at[5])
    prior_copy.start()
    acc[...] = jnp.full(acc.shape, 3e38, F32)
    slots_copy.wait()
    for load in loads:
        load.wait()

    first = slots_ref[0]
    for i in range(RA + RB):
        slot = slots_ref[i]
        own[0, i : i + 1, :] = pf[pl.ds(jnp.where(slot >= 0, slot, first), 1), :]

    pl.semaphore_wait(barrier, len(near))

    def up(t):
        return max(2 * t - 1, 0)

    def sent(kind, t):
        return ssem.at[kind, t % 2]

    parts = [pl.ds(i * (RA + RB) // SPLIT, (RA + RB) // SPLIT) for i in range(SPLIT)]

    def own_up(i, t):
        src, dst = own.at[up(t), parts[i]], own.at[2 * t + 1, parts[i]]
        return remote(src, dst, sent(i, t), rown.at[i, 0, t + 1], zu)

    def own_dn(i, t):
        src, dst = own.at[2 * t, parts[i]], own.at[2 * t + 2, parts[i]]
        return remote(src, dst, sent(2 + i, t), rown.at[i, 1, t + 1], zd)

    def all_up(t):
        return remote(ga.at[up(t)], ga.at[2 * t + 1], sent(4, t), rall.at[0, t + 1], zu)

    def all_dn(t):
        return remote(ga.at[2 * t], ga.at[2 * t + 2], sent(5, t), rall.at[1, t + 1], zd)

    def xr(t):
        two = pl.ds(2 * t - 1, 2)
        src = own.at[two, pl.ds(RA, RB)]
        return remote(src, gb.at[2, two], sent(6, t), rx.at[0, t], xu)

    def xl(t):
        two = pl.ds(2 * t - 1, 2)
        src = own.at[two, pl.ds(RA, RB)]
        return remote(src, gb.at[0, two], sent(7, t), rx.at[1, t], xd)

    def rel_r(t):
        at = 2 * t - 1
        return remote(gb.at[2, at], gb.at[1, at], sent(8, t), rr.at[0, t], xu)

    def rel_l(t):
        return remote(gb.at[0, 2 * t], gb.at[1, 2 * t], sent(9, t), rr.at[1, t], xd)

    around = (3, 1, 2)
    own_a = [
        remote(own.at[0, pl.ds(0, RA)], ga.at[0, d - 1], s0.at[i], rax.at[i], peer(0, -d))
        for i, d in enumerate(around)
    ]
    own_b = [
        remote(own.at[0, pl.ds(RA, RB)], gb.at[d - 1, 0], s0.at[3 + i], rbx.at[i], peer(0, -d))
        for i, d in enumerate(around)
    ]
    far = 2 * HALF - 1
    last_b = [
        remote(own.at[far, pl.ds(RA, RB)], gb.at[d - 1, far], s0.at[6 + i], rbx.at[3 + i], peer(0, -d))
        for i, d in enumerate(around)
    ]

    for copy in own_a:
        copy.start()
    for i in range(SPLIT):
        own_up(i, 0).start()
        own_dn(i, 0).start()
    for copy in own_b:
        copy.start()

    for q in range(npts // 256):
        cols = pl.ds(q * 256, 256)
        t = pf[cols, :].T
        pn[:, cols] = jnp.sum(t * t, axis=0, keepdims=True)
        t = t * -2.0
        hi = t.astype(BF16)
        lo = (t - hi.astype(F32)).astype(BF16)
        p3[0:width, cols] = hi
        p3[width : 2 * width, cols] = lo
        p3[2 * width : 3 * width, cols] = hi

    def fill(at, pieces):
        rows = pieces[0] if len(pieces) == 1 else jnp.concatenate(pieces, axis=0)
        n = rows.shape[0]
        sq = rows * rows
        sq = sum(sq[:, 128 * i : 128 * i + 128] for i in range(width // 128))
        cnb[at : at + n, :] = jnp.broadcast_to(jnp.sum(sq, axis=1, keepdims=True), (n, 128))
        hi = rows.astype(BF16)
        c3[at : at + n, 0:width] = hi
        c3[at : at + n, width : 2 * width] = hi
        c3[at : at + n, 2 * width : 3 * width] = (rows - hi.astype(F32)).astype(BF16)

    def nearest(at, n):
        d = jnp.dot(c3[at : at + n, :], p3[...], preferred_element_type=F32)
        d = d + jnp.concatenate([cnb[at : at + n, :]] * (npts // 128), axis=1)
        acc[...] = jnp.minimum(acc[...], jnp.min(d.reshape(n // 8, 8, npts), axis=0))

    def others(pos):
        return ga[pos].reshape((NX - 1) * RA, width)

    fill(208, [own[0], own[0, 0:16]])
    for copy in own_a:
        copy.wait_recv()
    all_dn(0).start()
    all_up(0).start()

    def tick(t, _):
        for i in range(SPLIT):
            own_up(i, t - 1).wait_recv()

            @when(t < HALF)
            def _():
                own_up(i, t).start()
                own_dn(i, t - 1).wait_recv()

            @when(t < HALF - 1)
            def _():
                own_dn(i, t).start()

        @when(t < HALF)
        def _():
            xr(t).start()
            xl(t).start()
            fill(0, [own[2 * t - 1], own[2 * t]])

        @when(t == HALF)
        def _():
            for copy in last_b:
                copy.start()
            fill(0, [own[far], own[far]])

        @when(t == 1)
        def _():
            for copy in own_b:
                copy.wait_recv()
            fill(64, [gb[0, 0], gb[1, 0], gb[2, 0], others(0)])

        @when(t >= 3)
        def _():
            fill(64, [gb[2, 2 * t - 5], gb[2, 2 * t - 4], gb[0, 2 * t - 5], gb[0, 2 * t - 4]])

        nearest(0, 160)

        @when(t == HALF)
        def _():
            relay(t - 1)

        all_dn(t - 1).wait_recv()

        @when(t < HALF)
        def _():
            all_dn(t).start()
            all_up(t - 1).wait_recv()

        @when(t < HALF - 1)
        def _():
            all_up(t).start()

        @when(t < HALF)
        def _():
            fill(160, [others(2 * t - 1), others(2 * t)])

        @when(t == HALF)
        def _():
            fill(160, [others(2 * HALF), others(2 * HALF)])

        @when(t >= 4)
        def _():
            rel_r(t - 3).wait_recv()
            rel_l(t - 3).wait_recv()
            fill(208, [gb[1, 2 * t - 7], gb[1, 2 * t - 6]])

        nearest(160, 96)

        @when(t >= 2 and t < HALF)
        def _():
            relay(t - 1)

        for i in range(SPLIT):
            own_up(i, t - 1).wait_send()
        all_dn(t - 1).wait_send()

        @when(t < HALF)
        def _():
            for i in range(SPLIT):
                own_dn(i, t - 1).wait_send()
            all_up(t - 1).wait_send()

        @when(t >= 2)
        def _():
            xr(t - 1).wait_send()
            xl(t - 1).wait_send()

        @when(t >= 3)
        def _():
            rel_r(t - 2).wait_send()
            rel_l(t - 2).wait_send()

        return 0

    def relay(t):
        xr(t).wait_recv()
        xl(t).wait_recv()
        rel_r(t).start()
        rel_l(t).start()

    for t in range(1, HALF + 1):
        tick(t, 0)

    fill(0, [gb[2, 13], gb[2, 14], gb[0, 13], gb[0, 14]])
    rel_r(HALF - 2).wait_recv()
    rel_l(HALF - 2).wait_recv()
    fill(96, [gb[1, 11], gb[1, 12]])
    nearest(0, 144)
    for copy in own_a + own_b:
        copy.wait_send()
    for copy in last_b:
        copy.wait_recv()
    rel_r(HALF - 1).wait_recv()
    rel_l(HALF - 1).wait_recv()
    fill(0, [gb[1, 13], gb[1, 14], gb[0, 15], gb[1, 15], gb[2, 15], gb[2, 15, 0:8]])
    nearest(0, 128)
    rel_r(HALF - 1).wait_send()
    rel_l(HALF - 1).wait_send()

    low = jnp.min(acc[...], axis=0, keepdims=True)
    low = (low + pn[...]) / width
    for i in range(npts // 128):
        mins[0, i : i + 1, :] = low[:, 128 * i : 128 * i + 128]
    swaps = [remote(mins.at[0], mins.at[j], scm.at[j], rcm.at[j], mate(j)) for j in range(1, NC)]
    for copy in swaps:
        copy.start()
    for copy in last_b:
        copy.wait_send()
    prior_copy.wait()
    new = jnp.minimum(prior_ref[...], mins[0])
    for copy in swaps:
        copy.wait_recv()
    for j in range(1, NC):
        new = jnp.minimum(new, mins[j])
    out_ref[...] = new

    sz[p] = jnp.sum(new, axis=0, keepdims=True)
    order = sorted(range(1, NZ * NX), key=lambda d: -(min(d // NX, NZ - d // NX) + min(d % NX, NX - d % NX)))

    def total_at(i, slot):
        d = order[i]
        return remote(sz.at[p], sz.at[slot], scz.at[i], rcz.at[i], peer(d // NX, d % NX))

    sums = [total_at(i, p) for i in range(NZ * NX - 1)]
    for copy in sums:
        copy.start()
    for copy in swaps:
        copy.wait_send()
    for copy in sums:
        copy.wait_send()
    for i, d in reversed(list(enumerate(order))):
        src = lax.rem(z - d // NX + NZ, NZ) * NX + lax.rem(x - d % NX + NX, NX)
        total_at(i, src).wait_recv()
    total = jnp.sum(sz[...], axis=0)
    cost_ref[...] = jnp.broadcast_to(
        jnp.sum(total, axis=1, keepdims=True) / (npts * NZ * NX), cost_ref.shape
    )


def hbm(array):
    return pltpu.with_memory_space_constraint(array, pltpu.HBM)


def local(points, prior_min, cand_slots):
    npts, width = points.shape
    vmem = pl.BlockSpec(memory_space=pltpu.VMEM)
    dma = pltpu.SemaphoreType.DMA
    new, cost = pl.pallas_call(
        kernel,
        out_shape=(
            jax.ShapeDtypeStruct((npts // 128, 128), F32),
            jax.ShapeDtypeStruct((1, 128), F32),
        ),
        in_specs=[pl.BlockSpec(memory_space=pltpu.HBM)] * 3,
        out_specs=(vmem, vmem),
        scratch_shapes=[
            pltpu.SMEM((RA + RB,), jnp.int32),
            pltpu.VMEM((npts // 128, 128), F32),
            pltpu.VMEM((npts, width), F32),
            pltpu.VMEM((3 * width, npts), BF16),
            pltpu.VMEM((1, npts), F32),
            pltpu.VMEM((NZ, RA + RB, width), F32),
            pltpu.VMEM((NZ + 1, NX - 1, RA, width), F32),
            pltpu.VMEM((NX - 1, NZ, RB, width), F32),
            pltpu.VMEM((256, 3 * width), BF16),
            pltpu.VMEM((256, 128), F32),
            pltpu.VMEM((8, npts), F32),
            pltpu.VMEM((NC, npts // 128, 128), F32),
            pltpu.VMEM((NZ * NX, 1, 128), F32),
            dma((6,)), dma((10, 2)),
            dma((SPLIT, 2, HALF + 1)), dma((2, HALF + 1)), dma((2, HALF + 1)), dma((2, HALF + 1)),
            dma((3,)), dma((6,)), dma((9,)),
            dma((NC,)), dma((NC,)), dma((NZ * NX,)), dma((NZ * NX,)),
        ],
        compiler_params=pltpu.CompilerParams(
            collective_id=0, has_side_effects=True, vmem_limit_bytes=48 << 20
        ),
    )(hbm(points), hbm(prior_min.reshape(npts // 128, 128)), hbm(cand_slots.reshape(-1)))
    return new.reshape(-1), cost[0, 0]


def solution(mesh):
    placed = (P("pts", None), P("pts"), P("pts", "cand", None))
    return jax.shard_map(
        local, mesh=mesh, in_specs=placed, out_specs=(P("pts"), P()), check_vma=False
    )
```
